768 devices in a mesh: dom: 96 (over z, x, core), mp: 8 (over y).
Axes of the slice: x: 4, y: 8, z: 12, core: 2. Of those that a mesh axis runs over, the one named last changes fastest.
Arguments:
- node_states: bfloat16 [49152, 1024], P(('dom', 'mp')), may hold values from -6 to 6
- edge_states: bfloat16 [147456, 1024], P(('dom', 'mp')), may hold values from -6 to 6
- edge_weight: bfloat16 [1024, 1024], P('mp'), may hold values from -0.109375 to 0.109375
- send_weight: bfloat16 [1024, 1024], P('mp'), may hold values from -0.109375 to 0.109375
- receive_weight: bfloat16 [1024, 1024], P('mp'), may hold values from -0.109375 to 0.109375
- output_weight: bfloat16 [1024, 1024], P('mp'), may hold values from -0.1875 to 0.1875
- norm_gain: float32 [1024], replicated, may hold values from 0.5 to 1.5
- senders: int32 [147456], P(('dom', 'mp')), may hold values from 0 to 127
- receivers: int32 [147456], P(('dom', 'mp')), may hold values from 0 to 63
- send_rows: int32 [768, 4, 16], P(('dom', 'mp')), may hold values from 0 to 63
- node_cotangent: bfloat16 [49152, 1024], P(('dom', 'mp')), may hold values from -6 to 6
- edge_cotangent: bfloat16 [147456, 1024], P(('dom', 'mp')), may hold values from -6 to 6
Outputs:
- new_nodes: bfloat16 [49152, 1024], P(('dom', 'mp'))
- new_edges: bfloat16 [147456, 1024], P(('dom', 'mp'))
- grad_nodes: bfloat16 [49152, 1024], P(('dom', 'mp'))
- grad_edges: bfloat16 [147456, 1024], P(('dom', 'mp'))
The draws below stay inside these ranges and needn't reach their ends.
Inputs may be any that keep to these rules, and one draw needn't show every extreme that they name: `senders`: A table row of the edge's own block. `receivers`: A node of the edge's own block. `send_rows`: local node indices of the sending block; a node may be listed more than once.
All inputs are finite; a program needn't handle non-finite values.
Results may differ from the reference program's by a relative error of at most 0.0059.
Values may be sent and summed in bfloat16 or wider, within the bound.
No kernel may reach another device: no remote copies, remote signals or barrier semaphores. Data moves between devices by JAX's collectives and lax.ppermute only.
A program may use at most 32 MiB of HBM per device.

```python
import jax
import jax.numpy as jnp
from jax import lax

D = 1024
F = 1024
N_DEV = 64
SPAN = 2
HALO = 16
E_DEV = 192
TABLE = 128
BLOCKS = 768
NODES = 49152
EDGES = 147456


def touch_ends(array, own_key, smallest, top_value):
    spot = [jax.random.randint(jax.random.fold_in(own_key, axis), (), 0, length) for axis, length in enumerate(array.shape)]
    widest = array.shape.index(max(array.shape))
    next_to = spot[:widest] + [(spot[widest] + 1) % array.shape[widest]] + spot[widest + 1:]
    return array.at[tuple(spot)].set(smallest).at[tuple(next_to)].set(top_value)


def block_scale(rng, shape, split, low, largest):
    factor_of = 1.0
    for position, blocks in split:
        draws = jax.random.uniform(jax.random.fold_in(jax.random.fold_in(rng, 6), position), (blocks,), jnp.float32, low / len(split), largest / len(split))
        factor_of = factor_of * jnp.repeat(jnp.exp(draws), shape[position] // blocks).reshape((-1,) + (1,) * (len(shape) - 1 - position))
    return factor_of


def normal_values(rng, shape, scale, limit, cuts=(), kind=jnp.bfloat16):
    array = jax.random.normal(rng, shape, jnp.float32) * scale
    if len(cuts) > 0:
        array = block_scale(rng, shape, cuts, -0.22, 0.18) * array
    return jnp.clip(array, min=-limit, max=limit).astype(kind)


def setup_inputs(seed: int = 0) -> dict:
    key_of = jax.random.split(jax.random.key(seed), 13)
    node_states = normal_values(key_of[0], (NODES, D), 1.0, 6.0, ((0, 768),))
    edge_states = normal_values(key_of[1], (EDGES, D), 1.0, 6.0, ((0, 768),))
    edge_weight = normal_values(key_of[2], (D, F), (3 * D) ** -0.5, 0.109375, ((0, 8),))
    send_weight = normal_values(key_of[3], (D, F), (3 * D) ** -0.5, 0.109375, ((0, 8),))
    receive_weight = normal_values(key_of[4], (D, F), (3 * D) ** -0.5, 0.109375, ((0, 8),))
    output_weight = normal_values(key_of[5], (F, D), F ** -0.5, 0.1875, ((0, 8),))
    norm_gain = jnp.clip(1.0 + 0.1 * jax.random.normal(key_of[6], (D,), jnp.float32), 0.5, 1.5)
    senders = touch_ends(jax.random.randint(key_of[7], (EDGES,), 0, TABLE), jax.random.fold_in(key_of[7], 1), 0, TABLE - 1).astype(jnp.int32)
    receivers = touch_ends(jax.random.randint(key_of[8], (EDGES,), 0, N_DEV), jax.random.fold_in(key_of[8], 1), 0, N_DEV - 1).astype(jnp.int32)
    send_rows = touch_ends(jax.random.randint(key_of[9], (BLOCKS, 2 * SPAN, HALO), 0, N_DEV), jax.random.fold_in(key_of[9], 1), 0, N_DEV - 1).astype(jnp.int32)
    node_cotangent = normal_values(key_of[10], (NODES, D), 1.0, 6.0, ((0, 768),))
    edge_cotangent = normal_values(key_of[11], (EDGES, D), 1.0, 6.0, ((0, 768),))
    return dict(node_states=node_states, edge_states=edge_states, edge_weight=edge_weight, send_weight=send_weight, receive_weight=receive_weight, output_weight=output_weight, norm_gain=norm_gain, senders=senders, receivers=receivers, send_rows=send_rows, node_cotangent=node_cotangent, edge_cotangent=edge_cotangent)


eps = 1e-05

def normalize(values, norm_gain):
    average = lax.optimization_barrier(jnp.mean(values, axis=-1, keepdims=True))
    centred = values - average
    variance = lax.optimization_barrier(jnp.mean(centred * centred, axis=-1, keepdims=True))
    return centred * lax.rsqrt(variance + eps) * norm_gain.astype(jnp.float32)

def silu_slope(preact):
    sigmoid_value = jax.nn.sigmoid(preact)
    return sigmoid_value * (1.0 + preact * (1.0 - sigmoid_value))

def shift_list(spread):
    return [stride + 1 for stride in range(spread)] + [-(stride + 1) for stride in range(spread)]

def pick_rows(block_rows, row_ids):
    return jnp.take(block_rows, row_ids, axis=0)

def add_rows(totals, row_ids, values):
    return totals.at[row_ids].add(values)

def reference(node_states, edge_states, edge_weight, send_weight, receive_weight, output_weight, norm_gain, senders, receivers, send_rows, node_cotangent, edge_cotangent):
    blocks = node_states.shape[0] // N_DEV
    feature = node_states.shape[1]
    shifts = shift_list(SPAN)
    send_projection = jnp.dot(node_states, send_weight, preferred_element_type=jnp.float32).astype(jnp.bfloat16).reshape(blocks, N_DEV, F)
    receive_projection = jnp.dot(node_states, receive_weight, preferred_element_type=jnp.float32).astype(jnp.bfloat16).reshape(blocks, N_DEV, F)
    pieces = [send_projection]
    for block_index in range(2 * SPAN):
        chosen = jax.vmap(pick_rows)(send_projection, send_rows[:, block_index])
        pieces.append(jnp.roll(chosen, shifts[block_index], axis=0))
    lookup = jnp.concatenate(pieces, axis=1)

    def apply_norm(values):
        return normalize(values, norm_gain)

    def one_block(inputs):
        edge_block, lookup_block, receive_block, sender_ids, receiver_ids, node_block, node_grad, edge_grad = inputs
        preact = jnp.dot(edge_block, edge_weight, preferred_element_type=jnp.float32)
        preact = preact + jnp.take(lookup_block, sender_ids, axis=0).astype(jnp.float32)
        preact = preact + jnp.take(receive_block, receiver_ids, axis=0).astype(jnp.float32)
        hidden = jax.nn.silu(preact).astype(jnp.bfloat16)
        projected = jnp.dot(hidden, output_weight, preferred_element_type=jnp.float32)
        update, norm_back = jax.vjp(apply_norm, projected)
        new_edge = (edge_block.astype(jnp.float32) + update).astype(jnp.bfloat16)
        summed = jax.ops.segment_sum(new_edge.astype(jnp.float32), receiver_ids, num_segments=N_DEV)
        new_node = (node_block.astype(jnp.float32) + summed).astype(jnp.bfloat16)
        grad_total = edge_grad.astype(jnp.float32) + jnp.take(node_grad, receiver_ids, axis=0).astype(jnp.float32)
        grad_projected = norm_back(grad_total)[0].astype(jnp.bfloat16)
        grad_hidden = jnp.dot(grad_projected, output_weight.T, preferred_element_type=jnp.float32)
        grad_preact = (grad_hidden * silu_slope(preact)).astype(jnp.bfloat16)
        grad_edge = (grad_total + jnp.dot(grad_preact, edge_weight.T, preferred_element_type=jnp.float32)).astype(jnp.bfloat16)
        grad_lookup = jax.ops.segment_sum(grad_preact.astype(jnp.float32), sender_ids, num_segments=TABLE)
        grad_receive = jax.ops.segment_sum(grad_preact.astype(jnp.float32), receiver_ids, num_segments=N_DEV).astype(jnp.bfloat16)
        return (new_edge, new_node, grad_edge, grad_lookup[:N_DEV], grad_lookup[N_DEV:].astype(jnp.bfloat16), grad_receive)
    outputs = lax.map(one_block, (edge_states.reshape(blocks, E_DEV, feature), lookup, receive_projection, senders.reshape(blocks, E_DEV), receivers.reshape(blocks, E_DEV), node_states.reshape(blocks, N_DEV, feature), node_cotangent.reshape(blocks, N_DEV, feature), edge_cotangent.reshape(blocks, E_DEV, feature)))
    new_edges, new_nodes, grad_edges, own_grad, halo_grad, grad_receive = outputs
    halo_grad = halo_grad.reshape(blocks, 2 * SPAN, HALO, F)
    grad_send = own_grad
    for block_index in range(2 * SPAN):
        returned = jnp.roll(halo_grad[:, block_index], -shifts[block_index], axis=0).astype(jnp.float32)
        grad_send = jax.vmap(add_rows)(grad_send, send_rows[:, block_index], returned)
    grad_send = grad_send.astype(jnp.bfloat16).reshape(-1, F)
    grad_nodes = node_cotangent.astype(jnp.float32)
    grad_nodes = grad_nodes + jnp.dot(grad_send, send_weight.T, preferred_element_type=jnp.float32)
    grad_nodes = grad_nodes + jnp.dot(grad_receive.reshape(-1, F), receive_weight.T, preferred_element_type=jnp.float32)
    return (new_nodes.reshape(-1, feature), new_edges.reshape(-1, feature), grad_nodes.astype(jnp.bfloat16), grad_edges.reshape(-1, feature))
```

```python
import jax
import jax.numpy as jnp
from jax import lax
from jax.experimental import pallas as pl
from jax.experimental.pallas import tpu as pltpu
from jax.sharding import Mesh, PartitionSpec as P

eps = 1e-05
BF = jnp.bfloat16
F32 = jnp.float32
AXES = ("rest", "core", "mp")
EDGE, SEND, RECEIVE, OUTPUT = 0, 1, 2, 3
VMEM_BYTES = 48 * 1024 * 1024


def dot(left, right):
    return jnp.dot(left, right, preferred_element_type=F32)


def dot_rows(left, right):
    return lax.dot_general(left, right, (((1,), (1,)), ((), ())), preferred_element_type=F32)


def fetches(panels, held, sems, which):
    return [
        pltpu.make_async_copy(panels.at[core, :, which], held.at[:, core], sems.at[core])
        for core in range(2)
    ]


def begin(copies):
    for copy in copies:
        copy.start()


def finish(copies):
    for copy in copies:
        copy.wait()


def matrix(held):
    value = held[...]
    return value.reshape(-1, value.shape[-1])


def one_hot(ids_column, count):
    rows = ids_column.shape[0]
    return (lax.broadcasted_iota(jnp.int32, (rows, count), 1) == ids_column).astype(F32).astype(BF)


def one_hot_t(ids_row, count):
    columns = ids_row.shape[1]
    return (lax.broadcasted_iota(jnp.int32, (count, columns), 0) == ids_row).astype(F32).astype(BF)


def edge_kernel(
    panels, nodes, halo, edges, gain, send_col, recv_col, send_row, recv_row, node_cot, edge_cot,
    new_edges, grad_pre, own, halo_grad, grad_recv,
    w_send, w_recv, w_edge, w_out, sems,
):
    order = ((w_send, SEND), (w_recv, RECEIVE), (w_edge, EDGE), (w_out, OUTPUT))
    copies = [fetches(panels, held, sems.at[i], which) for i, (held, which) in enumerate(order)]
    for pair in copies:
        begin(pair)
    node_count = nodes.shape[0]
    table = node_count + halo.shape[0]
    pick_recv = one_hot(recv_col[...], node_count)
    grad_total = edge_cot[...].astype(F32) + dot(pick_recv, node_cot[...])
    finish(copies[0])
    lookup = dot(jnp.concatenate([nodes[...], halo[...]], axis=0), matrix(w_send)).astype(BF)
    finish(copies[1])
    received = dot(nodes[...], matrix(w_recv)).astype(BF)
    finish(copies[2])
    preact = dot(edges[...], matrix(w_edge))
    preact = preact + dot(one_hot(send_col[...], table), lookup)
    preact = preact + dot(pick_recv, received)
    gate = 1.0 / (1.0 + jnp.exp(-preact))
    hidden = (preact * gate).astype(BF)
    slope = gate * (1.0 + preact * (1.0 - gate))
    finish(copies[3])
    projected = dot(hidden, matrix(w_out))
    centred = projected - jnp.mean(projected, axis=-1, keepdims=True)
    scale = lax.rsqrt(jnp.mean(centred * centred, axis=-1, keepdims=True) + eps)
    normal = centred * scale
    new_edges[...] = (edges[...].astype(F32) + normal * gain[...]).astype(BF)
    pulled = grad_total * gain[...]
    mean_pulled = jnp.mean(pulled, axis=-1, keepdims=True)
    mean_along = jnp.mean(pulled * normal, axis=-1, keepdims=True)
    grad_projected = (scale * (pulled - mean_pulled - normal * mean_along)).astype(BF)
    grad_preact = (dot_rows(grad_projected, matrix(w_out)) * slope).astype(BF)
    grad_pre[...] = grad_preact
    grad_lookup = dot(one_hot_t(send_row[...], table), grad_preact)
    own[...] = grad_lookup[:node_count]
    halo_grad[...] = grad_lookup[node_count:].astype(BF)
    grad_recv[...] = dot(one_hot_t(recv_row[...], node_count), grad_preact).astype(BF)


def local_kernel(
    panels, nodes, new_edges, grad_pre, grad_recv, recv_col, recv_row, node_cot, edge_cot,
    new_nodes, grad_edges, part, w_edge, w_recv, sems,
):
    copies = [fetches(panels, w_edge, sems.at[0], EDGE), fetches(panels, w_recv, sems.at[1], RECEIVE)]
    for pair in copies:
        begin(pair)
    node_count = nodes.shape[0]
    summed = dot(one_hot_t(recv_row[...], node_count), new_edges[...])
    new_nodes[...] = (nodes[...].astype(F32) + summed).astype(BF)
    grad_total = edge_cot[...].astype(F32) + dot(one_hot(recv_col[...], node_count), node_cot[...])
    finish(copies[0])
    grad_edges[...] = (grad_total + dot_rows(grad_pre[...], matrix(w_edge))).astype(BF)
    finish(copies[1])
    part[...] = node_cot[...].astype(F32) + dot_rows(grad_recv[...], matrix(w_recv))


def node_kernel(panels, own, part, back_0, back_1, back_2, back_3, rows_row, grad_nodes, w_send, sems):
    copies = fetches(panels, w_send, sems, SEND)
    begin(copies)
    returned = jnp.concatenate([back_0[...], back_1[...], back_2[...], back_3[...]], axis=0)
    placed = dot(one_hot_t(rows_row[...], own.shape[0]), returned)
    grad_send = (own[...] + placed).astype(BF)
    finish(copies)
    grad_nodes[...] = (part[...] + dot_rows(grad_send, matrix(w_send))).astype(BF)


def run(kernel, outs, scratch, flops, panels, *values):
    return pl.pallas_call(
        kernel,
        out_shape=outs,
        in_specs=[pl.BlockSpec(memory_space=pl.ANY)]
        + [pl.BlockSpec(memory_space=pltpu.VMEM)] * len(values),
        out_specs=jax.tree.map(lambda _: pl.BlockSpec(memory_space=pltpu.VMEM), outs),
        scratch_shapes=scratch,
        compiler_params=pltpu.CompilerParams(vmem_limit_bytes=VMEM_BYTES),
        cost_estimate=pl.CostEstimate(flops=flops, bytes_accessed=8 * 2**20, transcendentals=0),
    )(panels, *values)


def shards(
    node_states,
    edge_states,
    edge_weight,
    send_weight,
    receive_weight,
    output_weight,
    norm_gain,
    senders,
    receivers,
    send_rows,
    node_cotangent,
    edge_cotangent,
):
    nodes, width = node_states.shape
    edges = edge_states.shape[0]
    spread, halo = send_rows.shape[1] // 2, send_rows.shape[2]
    shifts = [step + 1 for step in range(spread)] + [-(step + 1) for step in range(spread)]
    blocks = lax.axis_size(AXES)
    groups = lax.axis_size("mp")
    panel = edge_weight.shape[0] // 2
    core = lax.axis_index("core")

    def moved(value, steps):
        return lax.ppermute(value, AXES, [(i, (i + steps) % blocks) for i in range(blocks)])

    weights = jnp.stack([edge_weight, send_weight, receive_weight, output_weight])
    mine = lax.dynamic_slice_in_dim(weights, core * panel, panel, axis=1)
    gathered = lax.all_gather(mine.reshape(4 * panel, -1), ("core", "mp"), axis=0, tiled=True)
    panels = gathered.reshape(2, groups, 4, panel, -1)
    chosen = node_states.at[send_rows.reshape(-1)].get(mode="promise_in_bounds")
    arrived = [moved(chosen[j * halo : (j + 1) * halo], shifts[j]) for j in range(2 * spread)]
    halo_nodes = jnp.concatenate(arrived, axis=0)
    gain = norm_gain.reshape(1, -1)
    send_col, send_row = senders.reshape(-1, 1), senders.reshape(1, -1)
    recv_col, recv_row = receivers.reshape(-1, 1), receivers.reshape(1, -1)
    held = pltpu.VMEM((groups, 2, panel, width), BF)

    def rows(count, kind=BF):
        return jax.ShapeDtypeStruct((count, width), kind)

    new_edges, grad_pre, own, halo_grad, grad_recv = run(
        edge_kernel,
        (rows(edges), rows(edges), rows(nodes, F32), rows(2 * spread * halo), rows(nodes)),
        [held, held, held, held, pltpu.SemaphoreType.DMA((4, 2))],
        2 * 768 * width * width,
        panels, node_states, halo_nodes, edge_states, gain, send_col, recv_col, send_row, recv_row,
        node_cotangent, edge_cotangent,
    )
    back = [moved(halo_grad[j * halo : (j + 1) * halo], -shifts[j]) for j in range(2 * spread)]
    new_nodes, grad_edges, part = run(
        local_kernel,
        (rows(nodes), rows(edges), rows(nodes, F32)),
        [held, held, pltpu.SemaphoreType.DMA((2, 2))],
        2 * 256 * width * width,
        panels, node_states, new_edges, grad_pre, grad_recv, recv_col, recv_row, node_cotangent, edge_cotangent,
    )
    grad_nodes = run(
        node_kernel,
        rows(nodes),
        [held, pltpu.SemaphoreType.DMA((2,))],
        2 * 64 * width * width,
        panels, own, part, *back, send_rows.reshape(1, -1),
    )
    return new_nodes, new_edges, grad_nodes, grad_edges


def solution(mesh):
    split = Mesh(mesh.devices.reshape(-1, 2, mesh.shape["mp"]), AXES)
    rows_spec, panel_spec = P(AXES, None), P("mp", None)
    in_specs = (
        rows_spec,
        rows_spec,
        panel_spec,
        panel_spec,
        panel_spec,
        panel_spec,
        P(),
        P(AXES),
        P(AXES),
        P(AXES, None, None),
        rows_spec,
        rows_spec,
    )
    return jax.shard_map(
        shards, mesh=split, in_specs=in_specs, out_specs=(rows_spec,) * 4, check_vma=False
    )
```

```python
import jax
import jax.numpy as jnp
from jax import lax
from jax.experimental import pallas as pl
from jax.experimental.pallas import tpu as pltpu
from jax.sharding import Mesh, PartitionSpec as P

eps = 1e-05
BF = jnp.bfloat16
F32 = jnp.float32
AXES = ("rest", "core", "mp")
EDGE, SEND, RECEIVE, OUTPUT = 0, 1, 2, 3
HBM = pl.BlockSpec(memory_space=pltpu.HBM)
VMEM_BYTES = 56 * 1024 * 1024


def dot(left, right):
    return jnp.dot(left, right, preferred_element_type=F32)


def dot_rows(left, right):
    return lax.dot_general(left, right, (((1,), (1,)), ((), ())), preferred_element_type=F32)


def fetches(panels, held, sems, which):
    return [
        pltpu.make_async_copy(panels.at[core, :, which], held.at[:, core], sems.at[core])
        for core in range(2)
    ]


def begin(copies):
    for copy in copies:
        copy.start()


def finish(copies):
    for copy in copies:
        copy.wait()


def matrix(held):
    value = held[...]
    return value.reshape(-1, value.shape[-1])


def one_hot_t(ids_row, count):
    columns = ids_row.shape[1]
    return (lax.broadcasted_iota(jnp.int32, (count, columns), 0) == ids_row).astype(F32).astype(BF)


def picked(hot, table):
    return lax.dot_general(hot, table, (((0,), (0,)), ((), ())), preferred_element_type=F32)


def loads(pairs, sems):
    return [pltpu.make_async_copy(s, d, sems.at[i]) for i, (s, d) in enumerate(pairs)]


def pick_kernel(nodes, send_rows, *outs):
    for j, out in enumerate(outs):
        out[...] = picked(one_hot_t(send_rows[j : j + 1], nodes.shape[0]), nodes[...]).astype(BF)


def edge_kernel(
    panels, nodes_in, halo_0, halo_1, halo_2, halo_3, edges_in, gain_in, send_row_in, recv_row_in, node_cot_in, edge_cot_in,
    new_nodes, new_edges, grad_pre, own, out_0, out_1, out_2, out_3, grad_recv,
    w_send, w_recv, w_edge, w_out, table_rows, edges, gain, send_row, recv_row, node_cot, edge_cot,
    sems, small_sems,
):
    node_count, halo = nodes_in.shape[0], halo_0.shape[0]
    table = table_rows.shape[0]
    first = [(nodes_in, table_rows.at[pl.ds(0, node_count)])]
    for j, rows in enumerate((halo_0, halo_1, halo_2, halo_3)):
        first.append((rows, table_rows.at[pl.ds(node_count + j * halo, halo)]))
    rest = [(recv_row_in, recv_row), (send_row_in, send_row), (node_cot_in, node_cot), (edge_cot_in, edge_cot)]
    rest += [(gain_in, gain), (edges_in, edges)]
    small = loads(first + rest, small_sems)
    order = ((w_send, SEND), (w_recv, RECEIVE), (w_edge, EDGE), (w_out, OUTPUT))
    copies = [fetches(panels, held, sems.at[i], which) for i, (held, which) in enumerate(order)]
    begin(small[: len(first)])
    begin(copies[0])
    begin(small[len(first) :])
    for pair in copies[1:]:
        begin(pair)
    finish(small[: len(first)])
    finish(copies[0])
    lookup = dot(table_rows[...], matrix(w_send)).astype(BF)
    finish(small[len(first) :])
    to_recv = one_hot_t(recv_row[...], node_count)
    to_send = one_hot_t(send_row[...], table)
    grad_total = edge_cot[...].astype(F32) + picked(to_recv, node_cot[...])
    finish(copies[1])
    received = dot(table_rows[:node_count], matrix(w_recv)).astype(BF)
    finish(copies[2])
    preact = dot(edges[...], matrix(w_edge))
    preact = preact + picked(to_send, lookup)
    preact = preact + picked(to_recv, received)
    gate = 1.0 / (1.0 + jnp.exp(-preact))
    hidden = (preact * gate).astype(BF)
    slope = gate * (1.0 + preact * (1.0 - gate))
    finish(copies[3])
    projected = dot(hidden, matrix(w_out))
    centred = projected - jnp.mean(projected, axis=-1, keepdims=True)
    scale = lax.rsqrt(jnp.mean(centred * centred, axis=-1, keepdims=True) + eps)
    normal = centred * scale
    edges_out = (edges[...].astype(F32) + normal * gain[...]).astype(BF)
    new_edges[...] = edges_out
    new_nodes[...] = (table_rows[:node_count].astype(F32) + dot(to_recv, edges_out)).astype(BF)
    pulled = grad_total * gain[...]
    mean_pulled = jnp.mean(pulled, axis=-1, keepdims=True)
    mean_along = jnp.mean(pulled * normal, axis=-1, keepdims=True)
    grad_projected = (scale * (pulled - mean_pulled - normal * mean_along)).astype(BF)
    grad_preact = (dot_rows(grad_projected, matrix(w_out)) * slope).astype(BF)
    grad_pre[...] = grad_preact
    grad_lookup = dot(to_send, grad_preact)
    own[...] = grad_lookup[:node_count]
    for j, out in enumerate((out_0, out_1, out_2, out_3)):
        out[...] = grad_lookup[node_count + j * halo : node_count + (j + 1) * halo].astype(BF)
    grad_recv[...] = dot(to_recv, grad_preact).astype(BF)


def local_kernel(
    panels, grad_pre_in, grad_recv_in, recv_row_in, node_cot_in, edge_cot_in, grad_edges, part,
    w_edge, w_recv, grad_pre, grad_recv, recv_row, node_cot, edge_cot, sems, small_sems,
):
    small = loads(
        ((grad_pre_in, grad_pre), (recv_row_in, recv_row), (node_cot_in, node_cot), (edge_cot_in, edge_cot),
         (grad_recv_in, grad_recv)),
        small_sems,
    )
    copies = [fetches(panels, w_edge, sems.at[0], EDGE), fetches(panels, w_recv, sems.at[1], RECEIVE)]
    begin(copies[0])
    begin(small)
    begin(copies[1])
    finish(small)
    to_recv = one_hot_t(recv_row[...], node_cot.shape[0])
    grad_total = edge_cot[...].astype(F32) + picked(to_recv, node_cot[...])
    finish(copies[0])
    grad_edges[...] = (grad_total + dot_rows(grad_pre[...], matrix(w_edge))).astype(BF)
    finish(copies[1])
    part[...] = node_cot[...].astype(F32) + dot_rows(grad_recv[...], matrix(w_recv))


def node_kernel(
    panels, own_in, part_in, rows_in, back_0, back_1, back_2, back_3, grad_nodes,
    w_send, own, part, rows, b_0, b_1, b_2, b_3, sems, small_sems,
):
    ins = (back_0, back_1, back_2, back_3, rows_in, own_in, part_in)
    small = loads(list(zip(ins, (b_0, b_1, b_2, b_3, rows, own, part))), small_sems)
    copies = fetches(panels, w_send, sems.at[0], SEND)
    begin(copies)
    begin(small)
    finish(small)
    grad_send = own[...]
    for j, back in enumerate((b_0, b_1, b_2, b_3)):
        grad_send = grad_send + dot(one_hot_t(rows[j : j + 1], own.shape[0]), back[...])
    finish(copies)
    grad_nodes[...] = (part[...] + dot_rows(grad_send.astype(BF), matrix(w_send))).astype(BF)


def run(kernel, outs, weights, flops, panels, values, kept):
    cores, groups, _, panel, width = panels.shape
    return pl.pallas_call(
        kernel,
        out_shape=outs,
        in_specs=[HBM] * (1 + len(values)),
        out_specs=jax.tree.map(lambda _: pl.BlockSpec(memory_space=pltpu.VMEM), outs),
        scratch_shapes=[pltpu.VMEM((groups, cores, panel, width), BF)] * weights
        + [pltpu.VMEM(k.shape, k.dtype) for k in kept]
        + [pltpu.SemaphoreType.DMA((weights, cores)), pltpu.SemaphoreType.DMA((len(values),))],
        compiler_params=pltpu.CompilerParams(vmem_limit_bytes=VMEM_BYTES),
        cost_estimate=pl.CostEstimate(flops=flops, bytes_accessed=4 * 2**20, transcendentals=0),
    )(panels, *values)


def shards(
    node_states,
    edge_states,
    edge_weight,
    send_weight,
    receive_weight,
    output_weight,
    norm_gain,
    senders,
    receivers,
    send_rows,
    node_cotangent,
    edge_cotangent,
):
    nodes, width = node_states.shape
    edges = edge_states.shape[0]
    spread, halo = send_rows.shape[1] // 2, send_rows.shape[2]
    shifts = [step + 1 for step in range(spread)] + [-(step + 1) for step in range(spread)]
    blocks = lax.axis_size(AXES)
    groups = lax.axis_size("mp")
    panel = edge_weight.shape[0] // 2
    core = lax.axis_index("core")

    def moved(value, steps):
        return lax.ppermute(value, AXES, [(i, (i + steps) % blocks) for i in range(blocks)])

    weights = jnp.stack([edge_weight, send_weight, receive_weight, output_weight])
    mine = lax.dynamic_slice_in_dim(weights, core * panel, panel, axis=1)
    gathered = lax.all_gather(mine.reshape(4 * panel, -1), ("core", "mp"), axis=0, tiled=True)
    panels = gathered.reshape(2, groups, 4, panel, -1)
    rows_by_shift = send_rows.reshape(2 * spread, halo)

    def rows(count, kind=BF):
        return jax.ShapeDtypeStruct((count, width), kind)

    halo_rows = (rows(halo),) * (2 * spread)
    chosen = pl.pallas_call(pick_kernel, out_shape=halo_rows)(node_states, rows_by_shift)
    arrived = [moved(chosen[j], shifts[j]) for j in range(2 * spread)]
    gain = norm_gain.reshape(1, -1)
    send_row, recv_row = senders.reshape(1, -1), receivers.reshape(1, -1)
    new_nodes, new_edges, grad_pre, own, *outgoing, grad_recv = run(
        edge_kernel,
        (rows(nodes), rows(edges), rows(edges), rows(nodes, F32), *halo_rows, rows(nodes)),
        4,
        2 * 768 * width * width,
        panels,
        [node_states, *arrived, edge_states, gain, send_row, recv_row, node_cotangent, edge_cotangent],
        [rows(nodes + 2 * spread * halo), edge_states, gain, send_row, recv_row, node_cotangent, edge_cotangent],
    )
    back = [moved(outgoing[j], -shifts[j]) for j in range(2 * spread)]
    near = [grad_pre, grad_recv, recv_row, node_cotangent, edge_cotangent]
    grad_edges, part = run(
        local_kernel, (rows(edges), rows(nodes, F32)), 2, 2 * 256 * width * width, panels, near, near
    )
    last = [own, part, rows_by_shift, *back]
    grad_nodes = run(
        node_kernel, rows(nodes), 1, 2 * 64 * width * width, panels, last, last
    )
    return new_nodes, new_edges, grad_nodes, grad_edges


def solution(mesh):
    split = Mesh(mesh.devices.reshape(-1, 2, mesh.shape["mp"]), AXES)
    rows_spec, panel_spec = P(AXES, None), P("mp", None)
    in_specs = (
        rows_spec,
        rows_spec,
        panel_spec,
        panel_spec,
        panel_spec,
        panel_spec,
        P(),
        P(AXES),
        P(AXES),
        P(AXES, None, None),
        rows_spec,
        rows_spec,
    )
    return jax.shard_map(
        shards, mesh=split, in_specs=in_specs, out_specs=(rows_spec,) * 4, check_vma=False
    )
```

```python
import jax
import jax.numpy as jnp
from jax import lax
from jax.experimental import pallas as pl
from jax.experimental.pallas import tpu as pltpu
from jax.sharding import Mesh, PartitionSpec as P

eps = 1e-05
BF = jnp.bfloat16
F32 = jnp.float32
AXES = ("rest", "core", "mp")
EDGE, SEND, RECEIVE, OUTPUT = 0, 1, 2, 3
HBM = pl.BlockSpec(memory_space=pltpu.HBM)
VMEM_BYTES = 56 * 1024 * 1024


def dot(left, right):
    return jnp.dot(left, right, preferred_element_type=F32)


def dot_rows(left, right):
    return lax.dot_general(left, right, (((1,), (1,)), ((), ())), preferred_element_type=F32)


def fetches(panels, held, sems, which):
    return [
        pltpu.make_async_copy(panels.at[core, :, which], held.at[:, core], sems.at[core])
        for core in range(2)
    ]


def begin(copies):
    for copy in copies:
        copy.start()


def finish(copies):
    for copy in copies:
        copy.wait()


def matrix(held):
    value = held[...]
    return value.reshape(-1, value.shape[-1])


def one_hot_t(ids_row, count):
    columns = ids_row.shape[1]
    return (lax.broadcasted_iota(jnp.int32, (count, columns), 0) == ids_row).astype(F32).astype(BF)


def picked(hot, table):
    return lax.dot_general(hot, table, (((0,), (0,)), ((), ())), preferred_element_type=F32)


def loads(pairs, sems):
    return [pltpu.make_async_copy(s, d, sems.at[i]) for i, (s, d) in enumerate(pairs)]


def pick_kernel(nodes, send_rows, *outs):
    for j, out in enumerate(outs):
        out[...] = picked(one_hot_t(send_rows[j : j + 1], nodes.shape[0]), nodes[...]).astype(BF)


def edge_kernel(
    panels, nodes_in, halo_0, halo_1, halo_2, halo_3, edges_in, gain_in, send_row_in, recv_row_in, node_cot_in, edge_cot_in,
    new_nodes, new_edges, grad_edges, own, out_0, out_1, out_2, out_3, part,
    w_send, w_recv, w_edge, w_out, table_rows, edges, gain, send_row, recv_row, node_cot, edge_cot,
    sems, small_sems,
):
    node_count, halo = nodes_in.shape[0], halo_0.shape[0]
    table = table_rows.shape[0]
    first = [(nodes_in, table_rows.at[pl.ds(0, node_count)])]
    for j, rows in enumerate((halo_0, halo_1, halo_2, halo_3)):
        first.append((rows, table_rows.at[pl.ds(node_count + j * halo, halo)]))
    rest = [(recv_row_in, recv_row), (send_row_in, send_row), (node_cot_in, node_cot), (edge_cot_in, edge_cot)]
    rest += [(gain_in, gain), (edges_in, edges)]
    small = loads(first + rest, small_sems)
    order = ((w_send, SEND), (w_recv, RECEIVE), (w_edge, EDGE), (w_out, OUTPUT))
    copies = [fetches(panels, held, sems.at[i], which) for i, (held, which) in enumerate(order)]
    begin(small)
    begin(copies[0])
    begin(copies[1])
    finish(small)
    to_recv = one_hot_t(recv_row[...], node_count)
    to_send = one_hot_t(send_row[...], table)
    finish(copies[0])
    begin(copies[2])
    lookup = dot(table_rows[...], matrix(w_send)).astype(BF)
    finish(copies[1])
    begin(copies[3])
    received = dot(table_rows[:node_count], matrix(w_recv)).astype(BF)
    grad_total = edge_cot[...].astype(F32) + picked(to_recv, node_cot[...])
    finish(copies[2])
    preact = dot(edges[...], matrix(w_edge))
    preact = preact + picked(to_send, lookup)
    preact = preact + picked(to_recv, received)
    gate = 1.0 / (1.0 + jnp.exp(-preact))
    hidden = (preact * gate).astype(BF)
    slope = gate * (1.0 + preact * (1.0 - gate))
    finish(copies[3])
    projected = dot(hidden, matrix(w_out))
    centred = projected - jnp.mean(projected, axis=-1, keepdims=True)
    scale = lax.rsqrt(jnp.mean(centred * centred, axis=-1, keepdims=True) + eps)
    normal = centred * scale
    edges_out = (edges[...].astype(F32) + normal * gain[...]).astype(BF)
    new_edges[...] = edges_out
    new_nodes[...] = (table_rows[:node_count].astype(F32) + dot(to_recv, edges_out)).astype(BF)
    pulled = grad_total * gain[...]
    mean_pulled = jnp.mean(pulled, axis=-1, keepdims=True)
    mean_along = jnp.mean(pulled * normal, axis=-1, keepdims=True)
    grad_projected = (scale * (pulled - mean_pulled - normal * mean_along)).astype(BF)
    grad_preact = (dot_rows(grad_projected, matrix(w_out)) * slope).astype(BF)
    grad_lookup = dot(to_send, grad_preact)
    own[...] = grad_lookup[:node_count]
    for j, out in enumerate((out_0, out_1, out_2, out_3)):
        out[...] = grad_lookup[node_count + j * halo : node_count + (j + 1) * halo].astype(BF)
    grad_recv = dot(to_recv, grad_preact).astype(BF)
    part[...] = node_cot[...].astype(F32) + dot_rows(grad_recv, matrix(w_recv))
    grad_edges[...] = (grad_total + dot_rows(grad_preact, matrix(w_edge))).astype(BF)


def node_kernel(
    panels, own_in, part_in, rows_in, back_0, back_1, back_2, back_3, grad_nodes,
    w_send, own, part, rows, b_0, b_1, b_2, b_3, sems, small_sems,
):
    ins = (back_0, back_1, back_2, back_3, rows_in, own_in, part_in)
    small = loads(list(zip(ins, (b_0, b_1, b_2, b_3, rows, own, part))), small_sems)
    copies = fetches(panels, w_send, sems.at[0], SEND)
    begin(copies)
    begin(small)
    finish(small)
    grad_send = own[...]
    for j, back in enumerate((b_0, b_1, b_2, b_3)):
        grad_send = grad_send + dot(one_hot_t(rows[j : j + 1], own.shape[0]), back[...])
    finish(copies)
    grad_nodes[...] = (part[...] + dot_rows(grad_send.astype(BF), matrix(w_send))).astype(BF)


def run(kernel, outs, weights, flops, panels, values, kept):
    cores, groups, _, panel, width = panels.shape
    return pl.pallas_call(
        kernel,
        out_shape=outs,
        in_specs=[HBM] * (1 + len(values)),
        out_specs=jax.tree.map(lambda _: pl.BlockSpec(memory_space=pltpu.VMEM), outs),
        scratch_shapes=[pltpu.VMEM((groups, cores, panel, width), BF)] * weights
        + [pltpu.VMEM(k.shape, k.dtype) for k in kept]
        + [pltpu.SemaphoreType.DMA((weights, cores)), pltpu.SemaphoreType.DMA((len(values),))],
        compiler_params=pltpu.CompilerParams(vmem_limit_bytes=VMEM_BYTES),
        cost_estimate=pl.CostEstimate(flops=flops, bytes_accessed=4 * 2**20, transcendentals=0),
    )(panels, *values)


def shards(
    node_states,
    edge_states,
    edge_weight,
    send_weight,
    receive_weight,
    output_weight,
    norm_gain,
    senders,
    receivers,
    send_rows,
    node_cotangent,
    edge_cotangent,
):
    nodes, width = node_states.shape
    edges = edge_states.shape[0]
    spread, halo = send_rows.shape[1] // 2, send_rows.shape[2]
    shifts = [step + 1 for step in range(spread)] + [-(step + 1) for step in range(spread)]
    blocks = lax.axis_size(AXES)
    groups = lax.axis_size("mp")
    panel = edge_weight.shape[0] // 2
    core = lax.axis_index("core")

    def moved(value, steps):
        return lax.ppermute(value, AXES, [(i, (i + steps) % blocks) for i in range(blocks)])

    weights = jnp.stack([edge_weight, send_weight, receive_weight, output_weight])
    mine = lax.dynamic_slice_in_dim(weights, core * panel, panel, axis=1)
    gathered = lax.all_gather(mine.reshape(4 * panel, -1), ("core", "mp"), axis=0, tiled=True)
    panels = gathered.reshape(2, groups, 4, panel, -1)
    rows_by_shift = send_rows.reshape(2 * spread, halo)

    def rows(count, kind=BF):
        return jax.ShapeDtypeStruct((count, width), kind)

    halo_rows = (rows(halo),) * (2 * spread)
    chosen = pl.pallas_call(pick_kernel, out_shape=halo_rows)(node_states, rows_by_shift)
    arrived = [moved(chosen[j], shifts[j]) for j in range(2 * spread)]
    gain = norm_gain.reshape(1, -1)
    send_row, recv_row = senders.reshape(1, -1), receivers.reshape(1, -1)
    new_nodes, new_edges, grad_edges, own, *outgoing, part = run(
        edge_kernel,
        (rows(nodes), rows(edges), rows(edges), rows(nodes, F32), *halo_rows, rows(nodes, F32)),
        4,
        2 * 768 * width * width,
        panels,
        [node_states, *arrived, edge_states, gain, send_row, recv_row, node_cotangent, edge_cotangent],
        [rows(nodes + 2 * spread * halo), edge_states, gain, send_row, recv_row, node_cotangent, edge_cotangent],
    )
    back = [moved(outgoing[j], -shifts[j]) for j in range(2 * spread)]
    last = [own, part, rows_by_shift, *back]
    grad_nodes = run(
        node_kernel, rows(nodes), 1, 2 * 64 * width * width, panels, last, last
    )
    return new_nodes, new_edges, grad_nodes, grad_edges


def solution(mesh):
    split = Mesh(mesh.devices.reshape(-1, 2, mesh.shape["mp"]), AXES)
    rows_spec, panel_spec = P(AXES, None), P("mp", None)
    in_specs = (
        rows_spec,
        rows_spec,
        panel_spec,
        panel_spec,
        panel_spec,
        panel_spec,
        P(),
        P(AXES),
        P(AXES),
        P(AXES, None, None),
        rows_spec,
        rows_spec,
    )
    return jax.shard_map(
        shards, mesh=split, in_specs=in_specs, out_specs=(rows_spec,) * 4, check_vma=False
    )
```

```python
import functools

import jax
import jax.numpy as jnp
from jax import lax
from jax.experimental import pallas as pl
from jax.experimental.pallas import tpu as pltpu
from jax.sharding import Mesh, PartitionSpec as P

eps = 1e-05
BF = jnp.bfloat16
F32 = jnp.float32
AXES = ("rest", "core", "mp")
EDGE, SEND, RECEIVE, OUTPUT = 0, 1, 2, 3
HBM = pl.BlockSpec(memory_space=pltpu.HBM)
VMEM_BYTES = 56 * 1024 * 1024


def dot(left, right):
    return jnp.dot(left, right, preferred_element_type=F32)


def dot_rows(left, right):
    return lax.dot_general(left, right, (((1,), (1,)), ((), ())), preferred_element_type=F32)


def fetches(panels, held, sems, which):
    return [
        pltpu.make_async_copy(panels.at[core, :, which], held.at[:, core], sems.at[core])
        for core in range(2)
    ]


def begin(copies):
    for copy in copies:
        copy.start()


def finish(copies):
    for copy in copies:
        copy.wait()


def matrix(held):
    value = held[...]
    return value.reshape(-1, value.shape[-1])


def one_hot_t(ids_row, count):
    columns = ids_row.shape[1]
    return (lax.broadcasted_iota(jnp.int32, (count, columns), 0) == ids_row).astype(F32).astype(BF)


def picked(hot, table):
    return lax.dot_general(hot, table, (((0,), (0,)), ((), ())), preferred_element_type=F32)


def loads(pairs, sems):
    return [pltpu.make_async_copy(s, d, sems.at[i]) for i, (s, d) in enumerate(pairs)]


def pick_kernel(nodes, send_rows, *outs):
    for j, out in enumerate(outs):
        out[...] = picked(one_hot_t(send_rows[j : j + 1], nodes.shape[0]), nodes[...]).astype(BF)


def edge_kernel(
    panels, nodes_in, halo_0, halo_1, halo_2, halo_3, edges_in, gain_in, send_row_in, recv_row_in, node_cot_in, edge_cot_in,
    new_nodes, new_edges, grad_pre, own, out_0, out_1, out_2, out_3, grad_recv,
    w_send, w_recv, w_edge, w_out, table_rows, edges, gain, send_row, recv_row, node_cot, edge_cot,
    sems, small_sems,
):
    node_count, halo = nodes_in.shape[0], halo_0.shape[0]
    table = table_rows.shape[0]
    first = [(nodes_in, table_rows.at[pl.ds(0, node_count)])]
    for j, rows in enumerate((halo_0, halo_1, halo_2, halo_3)):
        first.append((rows, table_rows.at[pl.ds(node_count + j * halo, halo)]))
    rest = [(recv_row_in, recv_row), (send_row_in, send_row), (node_cot_in, node_cot), (edge_cot_in, edge_cot)]
    rest += [(gain_in, gain), (edges_in, edges)]
    small = loads(first + rest, small_sems)
    order = ((w_send, SEND), (w_recv, RECEIVE), (w_edge, EDGE), (w_out, OUTPUT))
    copies = [fetches(panels, held, sems.at[i], which) for i, (held, which) in enumerate(order)]
    begin(small)
    begin(copies[0])
    begin(copies[1])
    finish(small)
    to_recv = one_hot_t(recv_row[...], node_count)
    to_send = one_hot_t(send_row[...], table)
    finish(copies[0])
    begin(copies[2])
    lookup = dot(table_rows[...], matrix(w_send)).astype(BF)
    finish(copies[1])
    begin(copies[3])
    received = dot(table_rows[:node_count], matrix(w_recv)).astype(BF)
    grad_total = edge_cot[...].astype(F32) + picked(to_recv, node_cot[...])
    finish(copies[2])
    preact = dot(edges[...], matrix(w_edge))
    preact = preact + picked(to_send, lookup)
    preact = preact + picked(to_recv, received)
    gate = 1.0 / (1.0 + jnp.exp(-preact))
    hidden = (preact * gate).astype(BF)
    slope = gate * (1.0 + preact * (1.0 - gate))
    finish(copies[3])
    projected = dot(hidden, matrix(w_out))
    centred = projected - jnp.mean(projected, axis=-1, keepdims=True)
    scale = lax.rsqrt(jnp.mean(centred * centred, axis=-1, keepdims=True) + eps)
    normal = centred * scale
    edges_out = (edges[...].astype(F32) + normal * gain[...]).astype(BF)
    new_edges[...] = edges_out
    new_nodes[...] = (table_rows[:node_count].astype(F32) + dot(to_recv, edges_out)).astype(BF)
    pulled = grad_total * gain[...]
    mean_pulled = jnp.mean(pulled, axis=-1, keepdims=True)
    mean_along = jnp.mean(pulled * normal, axis=-1, keepdims=True)
    grad_projected = (scale * (pulled - mean_pulled - normal * mean_along)).astype(BF)
    grad_preact = (dot_rows(grad_projected, matrix(w_out)) * slope).astype(BF)
    grad_pre[...] = grad_preact
    grad_lookup = dot(to_send, grad_preact)
    own[...] = grad_lookup[:node_count]
    for j, out in enumerate((out_0, out_1, out_2, out_3)):
        out[...] = grad_lookup[node_count + j * halo : node_count + (j + 1) * halo].astype(BF)
    grad_recv[...] = dot(to_recv, grad_preact).astype(BF)


def local_kernel(
    panels, grad_pre_in, grad_recv_in, recv_row_in, node_cot_in, edge_cot_in, grad_edges, part,
    w_edge, w_recv, grad_pre, grad_recv, recv_row, node_cot, edge_cot, sems, small_sems,
):
    small = loads(
        ((grad_pre_in, grad_pre), (recv_row_in, recv_row), (node_cot_in, node_cot), (edge_cot_in, edge_cot),
         (grad_recv_in, grad_recv)),
        small_sems,
    )
    copies = [fetches(panels, w_edge, sems.at[0], EDGE), fetches(panels, w_recv, sems.at[1], RECEIVE)]
    begin(copies[0])
    begin(small)
    begin(copies[1])
    finish(small)
    to_recv = one_hot_t(recv_row[...], node_cot.shape[0])
    grad_total = edge_cot[...].astype(F32) + picked(to_recv, node_cot[...])
    finish(copies[0])
    grad_edges[...] = (grad_total + dot_rows(grad_pre[...], matrix(w_edge))).astype(BF)
    finish(copies[1])
    part[...] = node_cot[...].astype(F32) + dot_rows(grad_recv[...], matrix(w_recv))


def node_kernel(
    order, panels, own_in, part_in, rows_in, back_0, back_1, back_2, back_3, grad_nodes,
    w_send, own, part, rows, b_0, b_1, b_2, b_3, sems, small_sems,
):
    ins = (back_0, back_1, back_2, back_3, rows_in, own_in, part_in)
    small = loads(list(zip(ins, (b_0, b_1, b_2, b_3, rows, own, part))), small_sems)
    copies = fetches(panels, w_send, sems.at[0], SEND)
    begin(copies)
    begin(small)
    finish(small)
    grad_send = own[...]
    for j, back in zip(order, (b_0, b_1, b_2, b_3)):
        grad_send = grad_send + dot(one_hot_t(rows[j : j + 1], own.shape[0]), back[...])
    finish(copies)
    grad_nodes[...] = (part[...] + dot_rows(grad_send.astype(BF), matrix(w_send))).astype(BF)


def run(kernel, outs, weights, flops, panels, values, kept):
    cores, groups, _, panel, width = panels.shape
    return pl.pallas_call(
        kernel,
        out_shape=outs,
        in_specs=[HBM] * (1 + len(values)),
        out_specs=jax.tree.map(lambda _: pl.BlockSpec(memory_space=pltpu.VMEM), outs),
        scratch_shapes=[pltpu.VMEM((groups, cores, panel, width), BF)] * weights
        + [pltpu.VMEM(k.shape, k.dtype) for k in kept]
        + [pltpu.SemaphoreType.DMA((weights, cores)), pltpu.SemaphoreType.DMA((len(values),))],
        compiler_params=pltpu.CompilerParams(vmem_limit_bytes=VMEM_BYTES),
        cost_estimate=pl.CostEstimate(flops=flops, bytes_accessed=4 * 2**20, transcendentals=0),
    )(panels, *values)


def shards(
    node_states,
    edge_states,
    edge_weight,
    send_weight,
    receive_weight,
    output_weight,
    norm_gain,
    senders,
    receivers,
    send_rows,
    node_cotangent,
    edge_cotangent,
):
    nodes, width = node_states.shape
    edges = edge_states.shape[0]
    spread, halo = send_rows.shape[1] // 2, send_rows.shape[2]
    shifts = [step + 1 for step in range(spread)] + [-(step + 1) for step in range(spread)]
    blocks = lax.axis_size(AXES)
    groups = lax.axis_size("mp")
    panel = edge_weight.shape[0] // 2
    core = lax.axis_index("core")

    def moved(value, steps):
        return lax.ppermute(value, AXES, [(i, (i + steps) % blocks) for i in range(blocks)])

    weights = jnp.stack([edge_weight, send_weight, receive_weight, output_weight])
    mine = lax.dynamic_slice_in_dim(weights, core * panel, panel, axis=1)
    gathered = lax.all_gather(mine.reshape(4 * panel, -1), ("core", "mp"), axis=0, tiled=True)
    panels = gathered.reshape(2, groups, 4, panel, -1)
    rows_by_shift = send_rows.reshape(2 * spread, halo)

    def rows(count, kind=BF):
        return jax.ShapeDtypeStruct((count, width), kind)

    halo_rows = (rows(halo),) * (2 * spread)
    chosen = pl.pallas_call(pick_kernel, out_shape=halo_rows)(node_states, rows_by_shift)
    arrived = [moved(chosen[j], shifts[j]) for j in range(2 * spread)]
    gain = norm_gain.reshape(1, -1)
    send_row, recv_row = senders.reshape(1, -1), receivers.reshape(1, -1)
    new_nodes, new_edges, grad_pre, own, *outgoing, grad_recv = run(
        edge_kernel,
        (rows(nodes), rows(edges), rows(edges), rows(nodes, F32), *halo_rows, rows(nodes)),
        4,
        2 * 768 * width * width,
        panels,
        [node_states, *arrived, edge_states, gain, send_row, recv_row, node_cotangent, edge_cotangent],
        [rows(nodes + 2 * spread * halo), edge_states, gain, send_row, recv_row, node_cotangent, edge_cotangent],
    )
    order = sorted(range(2 * spread), key=lambda j: (shifts[j] > 0, shifts[j]))
    back = [moved(outgoing[j], -shifts[j]) for j in order]
    near = [grad_pre, grad_recv, recv_row, node_cotangent, edge_cotangent]
    grad_edges, part = run(
        local_kernel, (rows(edges), rows(nodes, F32)), 2, 2 * 256 * width * width, panels, near, near
    )
    last = [own, part, rows_by_shift, *back]
    grad_nodes = run(
        functools.partial(node_kernel, order), rows(nodes), 1, 2 * 64 * width * width, panels, last, last
    )
    return new_nodes, new_edges, grad_nodes, grad_edges


def solution(mesh):
    split = Mesh(mesh.devices.reshape(-1, 2, mesh.shape["mp"]), AXES)
    rows_spec, panel_spec = P(AXES, None), P("mp", None)
    in_specs = (
        rows_spec,
        rows_spec,
        panel_spec,
        panel_spec,
        panel_spec,
        panel_spec,
        P(),
        P(AXES),
        P(AXES),
        P(AXES, None, None),
        rows_spec,
        rows_spec,
    )
    return jax.shard_map(
        shards, mesh=split, in_specs=in_specs, out_specs=(rows_spec,) * 4, check_vma=False
    )
```

```python
import functools

import jax
import jax.numpy as jnp
from jax import lax
from jax.experimental import pallas as pl
from jax.experimental.pallas import tpu as pltpu
from jax.sharding import Mesh, PartitionSpec as P

eps = 1e-05
BF = jnp.bfloat16
F32 = jnp.float32
AXES = ("rest", "core", "mp")
EDGE, SEND, RECEIVE, OUTPUT = 0, 1, 2, 3
HBM = pl.BlockSpec(memory_space=pltpu.HBM)
VMEM_BYTES = 56 * 1024 * 1024


def dot(left, right):
    return jnp.dot(left, right, preferred_element_type=F32)


def dot_rows(left, right):
    return lax.dot_general(left, right, (((1,), (1,)), ((), ())), preferred_element_type=F32)


def fetches(panels, held, sems, which):
    return [
        pltpu.make_async_copy(panels.at[core, :, which], held.at[:, core], sems.at[core])
        for core in range(2)
    ]


def begin(copies):
    for copy in copies:
        copy.start()


def finish(copies):
    for copy in copies:
        copy.wait()


def matrix(held):
    value = held[...]
    return value.reshape(-1, value.shape[-1])


def one_hot_t(ids_row, count):
    columns = ids_row.shape[1]
    return (lax.broadcasted_iota(jnp.int32, (count, columns), 0) == ids_row).astype(F32).astype(BF)


def picked(hot, table):
    return lax.dot_general(hot, table, (((0,), (0,)), ((), ())), preferred_element_type=F32)


def loads(pairs, sems):
    return [pltpu.make_async_copy(s, d, sems.at[i]) for i, (s, d) in enumerate(pairs)]


def pick_kernel(nodes, send_rows, *outs):
    for j, out in enumerate(outs):
        out[...] = picked(one_hot_t(send_rows[j : j + 1], nodes.shape[0]), nodes[...]).astype(BF)


def edge_kernel(
    panels, nodes_in, halo_0, halo_1, halo_2, halo_3, edges_in, gain_in, send_row_in, recv_row_in, node_cot_in, edge_cot_in,
    new_nodes, new_edges, grad_pre, own, out_0, out_1, out_2, out_3, part,
    w_send, w_recv, w_edge, w_out, table_rows, edges, gain, send_row, recv_row, node_cot, edge_cot,
    sems, small_sems,
):
    node_count, halo = nodes_in.shape[0], halo_0.shape[0]
    table = table_rows.shape[0]
    first = [(nodes_in, table_rows.at[pl.ds(0, node_count)])]
    for j, rows in enumerate((halo_0, halo_1, halo_2, halo_3)):
        first.append((rows, table_rows.at[pl.ds(node_count + j * halo, halo)]))
    rest = [(recv_row_in, recv_row), (send_row_in, send_row), (node_cot_in, node_cot), (edge_cot_in, edge_cot)]
    rest += [(gain_in, gain), (edges_in, edges)]
    small = loads(first + rest, small_sems)
    order = ((w_send, SEND), (w_recv, RECEIVE), (w_edge, EDGE), (w_out, OUTPUT))
    copies = [fetches(panels, held, sems.at[i], which) for i, (held, which) in enumerate(order)]
    begin(small)
    begin(copies[0])
    begin(copies[1])
    finish(small)
    to_recv = one_hot_t(recv_row[...], node_count)
    to_send = one_hot_t(send_row[...], table)
    finish(copies[0])
    begin(copies[2])
    lookup = dot(table_rows[...], matrix(w_send)).astype(BF)
    finish(copies[1])
    begin(copies[3])
    received = dot(table_rows[:node_count], matrix(w_recv)).astype(BF)
    grad_total = edge_cot[...].astype(F32) + picked(to_recv, node_cot[...])
    finish(copies[2])
    preact = dot(edges[...], matrix(w_edge))
    preact = preact + picked(to_send, lookup)
    preact = preact + picked(to_recv, received)
    gate = 1.0 / (1.0 + jnp.exp(-preact))
    hidden = (preact * gate).astype(BF)
    slope = gate * (1.0 + preact * (1.0 - gate))
    finish(copies[3])
    projected = dot(hidden, matrix(w_out))
    centred = projected - jnp.mean(projected, axis=-1, keepdims=True)
    scale = lax.rsqrt(jnp.mean(centred * centred, axis=-1, keepdims=True) + eps)
    normal = centred * scale
    edges_out = (edges[...].astype(F32) + normal * gain[...]).astype(BF)
    new_edges[...] = edges_out
    new_nodes[...] = (table_rows[:node_count].astype(F32) + dot(to_recv, edges_out)).astype(BF)
    pulled = grad_total * gain[...]
    mean_pulled = jnp.mean(pulled, axis=-1, keepdims=True)
    mean_along = jnp.mean(pulled * normal, axis=-1, keepdims=True)
    grad_projected = (scale * (pulled - mean_pulled - normal * mean_along)).astype(BF)
    grad_preact = (dot_rows(grad_projected, matrix(w_out)) * slope).astype(BF)
    grad_pre[...] = grad_preact
    grad_lookup = dot(to_send, grad_preact)
    own[...] = grad_lookup[:node_count]
    for j, out in enumerate((out_0, out_1, out_2, out_3)):
        out[...] = grad_lookup[node_count + j * halo : node_count + (j + 1) * halo].astype(BF)
    grad_recv = dot(to_recv, grad_preact).astype(BF)
    part[...] = node_cot[...].astype(F32) + dot_rows(grad_recv, matrix(w_recv))


def local_kernel(
    panels, grad_pre_in, recv_row_in, node_cot_in, edge_cot_in, grad_edges,
    w_edge, grad_pre, recv_row, node_cot, edge_cot, sems, small_sems,
):
    small = loads(
        ((recv_row_in, recv_row), (node_cot_in, node_cot), (edge_cot_in, edge_cot), (grad_pre_in, grad_pre)), small_sems
    )
    copies = fetches(panels, w_edge, sems.at[0], EDGE)
    begin(small)
    begin(copies)
    finish(small)
    to_recv = one_hot_t(recv_row[...], node_cot.shape[0])
    grad_total = edge_cot[...].astype(F32) + picked(to_recv, node_cot[...])
    finish(copies)
    grad_edges[...] = (grad_total + dot_rows(grad_pre[...], matrix(w_edge))).astype(BF)


def node_kernel(
    order, panels, own_in, part_in, rows_in, back_0, back_1, back_2, back_3, grad_nodes,
    w_send, own, part, rows, b_0, b_1, b_2, b_3, sems, small_sems,
):
    ins = (back_0, back_1, back_2, back_3, rows_in, own_in, part_in)
    small = loads(list(zip(ins, (b_0, b_1, b_2, b_3, rows, own, part))), small_sems)
    copies = fetches(panels, w_send, sems.at[0], SEND)
    begin(copies)
    begin(small)
    finish(small)
    grad_send = own[...]
    for j, back in zip(order, (b_0, b_1, b_2, b_3)):
        grad_send = grad_send + dot(one_hot_t(rows[j : j + 1], own.shape[0]), back[...])
    finish(copies)
    grad_nodes[...] = (part[...] + dot_rows(grad_send.astype(BF), matrix(w_send))).astype(BF)


def run(kernel, outs, weights, flops, panels, values, kept):
    cores, groups, _, panel, width = panels.shape
    return pl.pallas_call(
        kernel,
        out_shape=outs,
        in_specs=[HBM] * (1 + len(values)),
        out_specs=jax.tree.map(lambda _: pl.BlockSpec(memory_space=pltpu.VMEM), outs),
        scratch_shapes=[pltpu.VMEM((groups, cores, panel, width), BF)] * weights
        + [pltpu.VMEM(k.shape, k.dtype) for k in kept]
        + [pltpu.SemaphoreType.DMA((weights, cores)), pltpu.SemaphoreType.DMA((len(values),))],
        compiler_params=pltpu.CompilerParams(vmem_limit_bytes=VMEM_BYTES),
        cost_estimate=pl.CostEstimate(flops=flops, bytes_accessed=4 * 2**20, transcendentals=0),
    )(panels, *values)


def shards(
    node_states,
    edge_states,
    edge_weight,
    send_weight,
    receive_weight,
    output_weight,
    norm_gain,
    senders,
    receivers,
    send_rows,
    node_cotangent,
    edge_cotangent,
):
    nodes, width = node_states.shape
    edges = edge_states.shape[0]
    spread, halo = send_rows.shape[1] // 2, send_rows.shape[2]
    shifts = [step + 1 for step in range(spread)] + [-(step + 1) for step in range(spread)]
    blocks = lax.axis_size(AXES)
    groups = lax.axis_size("mp")
    panel = edge_weight.shape[0] // 2
    core = lax.axis_index("core")

    def moved(value, steps):
        return lax.ppermute(value, AXES, [(i, (i + steps) % blocks) for i in range(blocks)])

    weights = jnp.stack([edge_weight, send_weight, receive_weight, output_weight])
    mine = lax.dynamic_slice_in_dim(weights, core * panel, panel, axis=1)
    gathered = lax.all_gather(mine.reshape(4 * panel, -1), ("core", "mp"), axis=0, tiled=True)
    panels = gathered.reshape(2, groups, 4, panel, -1)
    rows_by_shift = send_rows.reshape(2 * spread, halo)

    def rows(count, kind=BF):
        return jax.ShapeDtypeStruct((count, width), kind)

    halo_rows = (rows(halo),) * (2 * spread)
    chosen = pl.pallas_call(pick_kernel, out_shape=halo_rows)(node_states, rows_by_shift)
    arrived = [moved(chosen[j], shifts[j]) for j in range(2 * spread)]
    gain = norm_gain.reshape(1, -1)
    send_row, recv_row = senders.reshape(1, -1), receivers.reshape(1, -1)
    new_nodes, new_edges, grad_pre, own, *outgoing, part = run(
        edge_kernel,
        (rows(nodes), rows(edges), rows(edges), rows(nodes, F32), *halo_rows, rows(nodes, F32)),
        4,
        2 * 768 * width * width,
        panels,
        [node_states, *arrived, edge_states, gain, send_row, recv_row, node_cotangent, edge_cotangent],
        [rows(nodes + 2 * spread * halo), edge_states, gain, send_row, recv_row, node_cotangent, edge_cotangent],
    )
    order = sorted(range(2 * spread), key=lambda j: (shifts[j] > 0, shifts[j]))
    back = [moved(outgoing[j], -shifts[j]) for j in order]
    near = [grad_pre, recv_row, node_cotangent, edge_cotangent]
    grad_edges = run(local_kernel, rows(edges), 1, 2 * 192 * width * width, panels, near, near)
    last = [own, part, rows_by_shift, *back]
    grad_nodes = run(
        functools.partial(node_kernel, order), rows(nodes), 1, 2 * 64 * width * width, panels, last, last
    )
    return new_nodes, new_edges, grad_nodes, grad_edges


def solution(mesh):
    split = Mesh(mesh.devices.reshape(-1, 2, mesh.shape["mp"]), AXES)
    rows_spec, panel_spec = P(AXES, None), P("mp", None)
    in_specs = (
        rows_spec,
        rows_spec,
        panel_spec,
        panel_spec,
        panel_spec,
        panel_spec,
        P(),
        P(AXES),
        P(AXES),
        P(AXES, None, None),
        rows_spec,
        rows_spec,
    )
    return jax.shard_map(
        shards, mesh=split, in_specs=in_specs, out_specs=(rows_spec,) * 4, check_vma=False
    )
```
